32 devices in a mesh: group: 2 (over y), src: 4 (over z), rcv: 4 (over x, core).
Axes of the slice: x: 2, y: 2, z: 4, core: 2. Of those that a mesh axis runs over, the one named last changes fastest.
Arguments:
- traces: bfloat16 [128, 36864], P(('group', 'src', 'rcv')), parts along dimension 0, may hold values from -6 to 6
- offsets: int32 [16], P('group'), parts along dimension 0, may hold values from 0 to 32768
- receiver_slots: int32 [8, 16], P(('group', 'rcv')), parts along dimension 0, may hold values from 0 to 15, each once within a row
Outputs:
- correlations: bfloat16 [128, 64, 128], P(('group', 'src'), 'rcv'), parts along dimension 0
The draws below stay inside these ranges and needn't reach their ends.
There are 2 independent parts, one for each index of `group`. The reference program is written for one: setup_inputs(seed, part) draws one part's arguments, and reference() takes and returns one part's arrays. A program takes and returns all parts, laid end to end along the dimension named above; each array names one. Nothing has to cross between parts.
All inputs are finite; a program needn't handle non-finite values.
Results may differ from the reference program's by a relative error of at most 0.0065.
Values may be sent and summed in bfloat16 or wider, within the bound.
A program may use at most 64 MiB of HBM per device.

```python
import math
import jax
import jax.numpy as jnp
from jax import lax

SEG_LEN = 4096
NB = 512
LAGS = 128
LAG_STEP = 4
SEGS = 8
CH_DEV = 4
WIN = 36864
SB = 16
RB = 16
CHANNELS = 64
N_RCV = 4


def place_ends(drawn, stream_key, smallest, high):
    spot = [jax.random.randint(jax.random.fold_in(stream_key, axis), (), 0, length) for axis, length in enumerate(drawn.shape)]
    longest = drawn.shape.index(max(drawn.shape))
    neighbour = spot[:longest] + [(spot[longest] + 1) % drawn.shape[longest]] + spot[longest + 1:]
    return drawn.at[tuple(spot)].set(smallest).at[tuple(neighbour)].set(high)


def shard_levels(key, shape, shards, low, top_value):
    def one(dim, shards_of):
        heights = jax.random.uniform(jax.random.fold_in(jax.random.fold_in(key, 6), dim), (shards_of,), jnp.float32, low / len(shards), top_value / len(shards))
        return jnp.repeat(jnp.exp(heights), shape[dim] // shards_of).reshape((-1,) + (1,) * (len(shape) - dim - 1))

    loudness = one(*shards[0])
    for cut in shards[1:]:
        loudness = loudness * one(*cut)
    return loudness


def centred(key, shape, spread, most, split=(), held_as=jnp.bfloat16):
    array = jax.random.normal(key, shape, jnp.float32) * spread
    if len(split) > 0:
        array = shard_levels(key, shape, split, -0.22, 0.18) * array
    return jnp.clip(array, min=-most, max=most).astype(held_as)


def setup_inputs(seed: int = 0, part: int = 0) -> dict:
    key_of = jax.random.split(jax.random.key(seed), 4)
    own_keys = jax.random.split(jax.random.fold_in(key_of[3], part), 4)
    traces = centred(own_keys[0], (CHANNELS, WIN), 1.0, 6.0, ((0, 16),))
    offsets = place_ends(jax.random.randint(own_keys[1], (SEGS,), 0, SEG_LEN * SEGS + 1), jax.random.fold_in(own_keys[1], 1), 0, SEG_LEN * SEGS).astype(jnp.int32)
    receiver_slots = jax.vmap(lambda own: jax.random.permutation(own, RB))(jax.random.split(own_keys[2], N_RCV)).reshape((N_RCV, RB)).astype(jnp.int32)
    return {"traces": traces, "offsets": offsets, "receiver_slots": receiver_slots}


def dft_table():
    t_index = jnp.arange(SEG_LEN, dtype=jnp.int32)[:, None]
    k_index = jnp.arange(NB, dtype=jnp.int32)[None, :]
    phase = jnp.mod(t_index * k_index, SEG_LEN).astype(jnp.float32) * (2.0 * math.pi / SEG_LEN)
    return jnp.concatenate([jnp.cos(phase), -jnp.sin(phase)], axis=1).astype(jnp.bfloat16)

def lag_table():
    k_index = jnp.arange(NB, dtype=jnp.int32)[:, None]
    lag_shift = LAG_STEP * (jnp.arange(LAGS, dtype=jnp.int32)[None, :] - LAGS // 2)
    phase = jnp.mod(k_index * lag_shift, SEG_LEN).astype(jnp.float32) * (2.0 * math.pi / SEG_LEN)
    return jnp.concatenate([jnp.cos(phase), -jnp.sin(phase)], axis=0).astype(jnp.bfloat16)

def whiten(traces, offsets):
    table = dft_table().astype(jnp.float32)
    pieces = jax.vmap(lambda start: lax.dynamic_slice_in_dim(traces, start, SEG_LEN, 1))(offsets)
    pieces = jnp.transpose(pieces, (1, 0, 2)).reshape(-1, SEG_LEN).astype(jnp.float32)
    spectra = jnp.dot(pieces, table, precision=lax.Precision.HIGHEST, preferred_element_type=jnp.float32)
    energy = lax.optimization_barrier(jnp.mean(spectra * spectra, axis=-1, keepdims=True))
    white = (spectra / jnp.sqrt(energy + 1e-06)).astype(jnp.bfloat16)
    return white.reshape(traces.shape[0], SEGS, 2 * NB)

def block_corr(sources, receivers, lags):
    high = lax.Precision.HIGHEST
    src_re = sources[..., :NB].astype(jnp.float32)
    src_im = sources[..., NB:].astype(jnp.float32)
    rec_re = receivers[..., :NB].astype(jnp.float32)
    rec_im = receivers[..., NB:].astype(jnp.float32)

    def pair(left, right):
        return jnp.einsum('sgk,rgk->srk', left, right, precision=high)
    real_part = pair(src_re, rec_re) + pair(src_im, rec_im)
    imag_part = pair(src_re, rec_im) - pair(src_im, rec_re)
    cross = jnp.concatenate([real_part, imag_part], axis=-1).astype(jnp.bfloat16)
    out = jnp.einsum('srk,kl->srl', cross.astype(jnp.float32), lags.astype(jnp.float32), precision=high)
    return (out * (1.0 / math.sqrt(SEGS * NB))).astype(jnp.bfloat16)

def reference(traces, offsets, receiver_slots):
    white = whiten(traces, offsets)
    column = jnp.arange(CHANNELS, dtype=jnp.int32)
    block_j = column // RB
    place = receiver_slots[block_j, column % RB]
    owner_i = place // CH_DEV
    within = place % CH_DEV
    channel = (owner_i * N_RCV + block_j) * CH_DEV + within
    receivers = white[channel]
    lags = lag_table()
    grouped = white.reshape(CHANNELS // SB, SB, SEGS, 2 * NB)
    out = lax.map(lambda blk: block_corr(blk, receivers, lags), grouped)
    return out.reshape(CHANNELS, CHANNELS, LAGS)
```

```python
import functools
import math

import jax
import jax.numpy as jnp
import numpy as np
from jax import lax
from jax.experimental import pallas as pl
from jax.experimental.pallas import tpu as pltpu
from jax.sharding import PartitionSpec as P

SEG_LEN = 4096
NB = 512
LAGS = 128
LAG_STEP = 4
RADIX = 4
FOLD = SEG_LEN // RADIX
BINS = NB // RADIX
MESH = pl.DeviceIdType.MESH


def tables():
    k = RADIX * np.arange(BINS)[None, :] + np.arange(RADIX)[:, None]
    t = np.arange(FOLD)[:, None, None]
    dft = 2.0 * math.pi / SEG_LEN * ((t * k[None]) % SEG_LEN)
    dft = np.stack([np.cos(dft), -np.sin(dft)], axis=2).reshape(FOLD, 2 * NB)
    tau = LAG_STEP * (np.arange(LAGS) - LAGS // 2)
    lag = 2.0 * math.pi / SEG_LEN * ((k[:, :, None] * tau) % SEG_LEN)
    lag = np.stack([np.cos(lag), -np.sin(lag)], axis=1).reshape(2 * NB, LAGS)
    return dft.astype(np.float32).astype(jnp.bfloat16), lag.astype(np.float32).astype(jnp.bfloat16)


def dot(left, right):
    return jnp.dot(left, right, preferred_element_type=jnp.float32)


def fold(segs, ch, offsets, traces, out, folded):
    window = traces.shape[1]
    lane = lax.broadcasted_iota(jnp.int32, (ch, 128), 1)
    for g in range(segs):
        start = offsets[g]
        shift = lax.rem(start, 128)
        base = pl.multiple_of(start - shift, 128)
        last = pl.multiple_of(jnp.minimum(base + SEG_LEN, window - 128), 128)
        main = traces[:, pl.ds(base, SEG_LEN)].astype(jnp.float32)
        extra = traces[:, pl.ds(last, 128)].astype(jnp.float32)
        back = lax.rem(128 - shift, 128)
        turned = [pltpu.roll(main[:, j * 128:(j + 1) * 128], back, 1) for j in range(SEG_LEN // 128)]
        turned.append(pltpu.roll(extra, back, 1))
        keep = lane < 128 - shift
        piece = [jnp.where(keep, turned[j], turned[j + 1]) for j in range(SEG_LEN // 128)]
        step = FOLD // 128
        here = slice(g * ch, (g + 1) * ch)
        for j in range(step):
            x0, x1, x2, x3 = (piece[q * step + j] for q in range(RADIX))
            even, odd = x0 + x2, x1 + x3
            at = slice(j * 128, (j + 1) * 128)
            folded[0, here, at] = even + odd
            folded[1, here, at] = even - odd
            folded[2, here, at] = x0 - x2
            folded[3, here, at] = x1 - x3
    out[...] = folded[...].astype(jnp.bfloat16)


def body(
    n_src, n_rcv, segs, ch,
    folded, dft, lag, corr,
    row_slots, col_slots, sources, receivers,
    row_send, row_recv, col_send, col_recv,
):
    me_r = lax.axis_index("rcv")
    me_s = lax.axis_index("src")
    rows = segs * ch

    barrier = pltpu.get_barrier_semaphore()
    for d in range(1, n_rcv):
        pl.semaphore_signal(barrier, inc=1, device_id={"rcv": lax.rem(me_r + d, n_rcv)}, device_id_type=MESH)

    def greet(d, _):
        pl.semaphore_signal(barrier, inc=1, device_id={"src": lax.rem(me_s + d, n_src)}, device_id_type=MESH)
        return 0

    lax.fori_loop(1, n_src, greet, 0)

    width = 2 * BINS
    p0 = dot(folded[0], dft[:, 0:width])
    p2 = dot(folded[1], dft[:, 2 * width:3 * width])
    both = folded[2:4].reshape(2 * rows, FOLD)
    p1 = dot(both, dft[:, width:2 * width])
    p3 = dot(both, dft[:, 3 * width:4 * width])
    parts = [
        p0[:, :BINS], p0[:, BINS:],
        p1[:rows, :BINS] + p1[rows:, BINS:], p1[:rows, BINS:] - p1[rows:, :BINS],
        p2[:, :BINS], p2[:, BINS:],
        p3[:rows, :BINS] - p3[rows:, BINS:], p3[:rows, BINS:] + p3[rows:, :BINS],
    ]
    spectra = jnp.concatenate(parts, axis=1)
    energy = jnp.sum(spectra * spectra, axis=1, keepdims=True) * (1.0 / (2 * NB))
    white = (spectra * (1.0 / jnp.sqrt(energy + 1e-06))).astype(jnp.bfloat16)
    row_slots[me_r] = white
    col_slots[me_s] = white

    pl.semaphore_wait(barrier, n_rcv - 1 + n_src - 1)

    def row_copy(to, slot):
        return pltpu.make_async_remote_copy(
            src_ref=row_slots.at[slot], dst_ref=row_slots.at[slot],
            send_sem=row_send.at[to], recv_sem=row_recv.at[slot],
            device_id={"rcv": to}, device_id_type=MESH,
        )

    def col_copy(to, slot):
        return pltpu.make_async_remote_copy(
            src_ref=col_slots.at[slot], dst_ref=col_slots.at[slot],
            send_sem=col_send.at[to], recv_sem=col_recv.at[slot],
            device_id={"src": to}, device_id_type=MESH,
        )

    for d in range(1, n_rcv):
        row_copy(lax.rem(me_r + d, n_rcv), me_r).start()

    def send(d, _):
        col_copy(lax.rem(me_s + d, n_src), me_s).start()
        return 0

    lax.fori_loop(1, n_src, send, 0)

    for d in range(1, n_rcv):
        other = lax.rem(me_r + d, n_rcv)
        row_copy(other, other).wait_recv()
    for j in range(n_rcv):
        block = row_slots[j].astype(jnp.float32)
        for g in range(segs):
            sources[g, j * ch:(j + 1) * ch, :] = block[g * ch:(g + 1) * ch]

    n_here = n_rcv * ch

    def shard(p):
        receivers[...] = col_slots[p].astype(jnp.float32)
        cross = []
        for r in range(RADIX):
            at_re = slice(r * width, r * width + BINS)
            at_im = slice(r * width + BINS, (r + 1) * width)
            re = im = 0.0
            for g in range(segs):
                s_re = sources[g, :, at_re][None]
                s_im = sources[g, :, at_im][None]
                r_re = receivers[g * ch:(g + 1) * ch, at_re][:, None]
                r_im = receivers[g * ch:(g + 1) * ch, at_im][:, None]
                re = re + (s_re * r_re + s_im * r_im)
                im = im + (s_re * r_im - s_im * r_re)
            cross += [re.astype(jnp.bfloat16).reshape(ch * n_here, BINS), im.astype(jnp.bfloat16).reshape(ch * n_here, BINS)]
        done = dot(jnp.concatenate(cross, axis=1), lag[...]) * (1.0 / math.sqrt(segs * NB))
        corr[pl.ds(p * ch, ch)] = done.reshape(ch, n_here, LAGS)

    shard(me_s)

    def arrive(d, _):
        other = lax.rem(me_s + d, n_src)
        col_copy(other, other).wait_recv()
        shard(other)
        return 0

    lax.fori_loop(1, n_src, arrive, 0)

    for d in range(1, n_rcv):
        row_copy(lax.rem(me_r + d, n_rcv), me_r).wait_send()

    def sent(d, _):
        col_copy(lax.rem(me_s + d, n_src), me_s).wait_send()
        return 0

    lax.fori_loop(1, n_src, sent, 0)


def arrange(slots, corr, out, placed):
    n_cols, n_here = corr.shape[:2]

    def place(q, _):
        tile = corr[slots[0, q]]
        for s in range(n_here):
            placed[s, pl.ds(q, 1), :] = tile[s:s + 1]
        return 0

    lax.fori_loop(0, n_cols, place, 0)
    out[...] = placed[...].astype(jnp.bfloat16)


def on_device(n_src, n_rcv, traces, offsets, receiver_slots):
    dft, lag = tables()
    ch = traces.shape[0]
    segs = offsets.shape[0]
    rows = segs * ch
    n_here, n_cols = n_rcv * ch, n_src * ch
    vmem = pl.BlockSpec(memory_space=pltpu.VMEM)
    smem = pl.BlockSpec(memory_space=pltpu.SMEM)
    room = 40 * 1024 * 1024
    folded = pl.pallas_call(
        functools.partial(fold, segs, ch),
        out_shape=jax.ShapeDtypeStruct((RADIX, rows, FOLD), jnp.bfloat16),
        in_specs=[smem, vmem],
        out_specs=vmem,
        scratch_shapes=[pltpu.VMEM((RADIX, rows, FOLD), jnp.float32)],
        compiler_params=pltpu.CompilerParams(vmem_limit_bytes=room),
    )(offsets, traces)
    corr = pl.pallas_call(
        functools.partial(body, n_src, n_rcv, segs, ch),
        out_shape=jax.ShapeDtypeStruct((n_cols, n_here, LAGS), jnp.float32),
        in_specs=[vmem] * 3,
        out_specs=vmem,
        scratch_shapes=[
            pltpu.VMEM((n_rcv, rows, 2 * NB), jnp.bfloat16),
            pltpu.VMEM((n_src, rows, 2 * NB), jnp.bfloat16),
            pltpu.VMEM((segs, n_here, 2 * NB), jnp.float32),
            pltpu.VMEM((rows, 2 * NB), jnp.float32),
            pltpu.SemaphoreType.DMA((n_rcv,)),
            pltpu.SemaphoreType.DMA((n_rcv,)),
            pltpu.SemaphoreType.DMA((n_src,)),
            pltpu.SemaphoreType.DMA((n_src,)),
        ],
        compiler_params=pltpu.CompilerParams(
            collective_id=0, has_side_effects=True, vmem_limit_bytes=room
        ),
    )(folded, jnp.asarray(dft), jnp.asarray(lag))
    return pl.pallas_call(
        arrange,
        out_shape=jax.ShapeDtypeStruct((n_here, n_cols, LAGS), jnp.bfloat16),
        in_specs=[smem, vmem],
        out_specs=vmem,
        scratch_shapes=[pltpu.VMEM((n_here, n_cols, LAGS), jnp.float32)],
        compiler_params=pltpu.CompilerParams(vmem_limit_bytes=room),
    )(receiver_slots, corr)


def solution(mesh):
    in_specs = (P(("group", "src", "rcv"), None), P("group"), P(("group", "rcv"), None))
    out_specs = P(("group", "src"), "rcv", None)
    return jax.shard_map(
        functools.partial(on_device, mesh.shape["src"], mesh.shape["rcv"]),
        mesh=mesh, in_specs=in_specs, out_specs=out_specs, check_vma=False,
    )
```

```python
import functools
import math

import jax
import jax.numpy as jnp
import numpy as np
from jax import lax
from jax.experimental import pallas as pl
from jax.experimental.pallas import tpu as pltpu
from jax.sharding import PartitionSpec as P

SEG_LEN = 4096
NB = 512
LAGS = 128
LAG_STEP = 4
RADIX = 4
FOLD = SEG_LEN // RADIX
BINS = NB // RADIX
MESH = pl.DeviceIdType.MESH


def tables():
    k = RADIX * np.arange(BINS)[None, :] + np.arange(RADIX)[:, None]
    t = np.arange(FOLD)[:, None, None]
    dft = 2.0 * math.pi / SEG_LEN * ((t * k[None]) % SEG_LEN)
    dft = np.stack([np.cos(dft), -np.sin(dft)], axis=2).reshape(FOLD, RADIX, 2 * BINS).transpose(1, 0, 2)
    tau = LAG_STEP * (np.arange(LAGS) - LAGS // 2)
    lag = 2.0 * math.pi / SEG_LEN * ((k[:, :, None] * tau) % SEG_LEN)
    lag = np.stack([np.cos(lag), -np.sin(lag)], axis=1).reshape(2 * NB, LAGS)
    return dft.astype(np.float32).astype(jnp.bfloat16), lag.astype(np.float32).astype(jnp.bfloat16)


def dot(left, right):
    return jnp.dot(left, right, preferred_element_type=jnp.float32)


def fold(segs, ch, offsets_in, slots_in, traces_in, out, pick, offsets, slots, traces, folded, chosen, in_sem):
    moves = [
        pltpu.make_async_copy(one, two, in_sem.at[i])
        for i, (one, two) in enumerate([(offsets_in, offsets), (slots_in, slots), (traces_in, traces)])
    ]
    for move in moves:
        move.start()
    for move in moves[:2]:
        move.wait()

    n_cols = chosen.shape[1]
    place = lax.broadcasted_iota(jnp.int32, (1, n_cols), 1)

    def choose(q, _):
        chosen[pl.ds(q, 1), :] = jnp.where(place == slots[0, q], 1.0, 0.0)
        return 0

    lax.fori_loop(0, n_cols, choose, 0)
    pick[...] = chosen[...].astype(jnp.bfloat16)
    moves[2].wait()
    window = traces.shape[1]
    lane = lax.broadcasted_iota(jnp.int32, (ch, 128), 1)
    for g in range(segs):
        start = offsets[g]
        shift = lax.rem(start, 128)
        base = pl.multiple_of(start - shift, 128)
        last = pl.multiple_of(jnp.minimum(base + SEG_LEN, window - 128), 128)
        main = traces[:, pl.ds(base, SEG_LEN)].astype(jnp.float32)
        extra = traces[:, pl.ds(last, 128)].astype(jnp.float32)
        back = lax.rem(128 - shift, 128)
        turned = [pltpu.roll(main[:, j * 128:(j + 1) * 128], back, 1) for j in range(SEG_LEN // 128)]
        turned.append(pltpu.roll(extra, back, 1))
        keep = lane < 128 - shift
        piece = [jnp.where(keep, turned[j], turned[j + 1]) for j in range(SEG_LEN // 128)]
        step = FOLD // 128
        here = slice(g * ch, (g + 1) * ch)
        for j in range(step):
            x0, x1, x2, x3 = (piece[q * step + j] for q in range(RADIX))
            even, odd = x0 + x2, x1 + x3
            at = slice(j * 128, (j + 1) * 128)
            folded[0, here, at] = even + odd
            folded[1, here, at] = even - odd
            folded[2, here, at] = x0 - x2
            folded[3, here, at] = x1 - x3
    out[...] = folded[...].astype(jnp.bfloat16)


def body(
    n_src, n_rcv, segs, ch,
    folded_in, pick_in, dft_in, lag_in, placed,
    folded, pick, dft, lag,
    row_slots, col_slots, sources, receivers, corr,
    in_sem, row_send, row_recv, col_send, col_recv,
):
    me_r = lax.axis_index("rcv")
    me_s = lax.axis_index("src")
    rows = segs * ch
    near = me_s + 1 - 2 * lax.rem(me_s, 2)
    across = n_src - 1 - me_s
    far = lax.rem(me_s + 2, n_src)
    inner = lax.rem(me_s, 3) != 0

    moves = [
        pltpu.make_async_copy(one, two, in_sem.at[i])
        for i, (one, two) in enumerate(
            [(folded_in, folded)] + [(dft_in.at[r], dft.at[r]) for r in range(RADIX)] + [(lag_in, lag), (pick_in, pick)]
        )
    ]
    for move in moves:
        move.start()

    barrier = pltpu.get_barrier_semaphore()
    for d in range(1, n_rcv):
        pl.semaphore_signal(barrier, inc=1, device_id={"rcv": lax.rem(me_r + d, n_rcv)}, device_id_type=MESH)

    def greet(d, _):
        pl.semaphore_signal(barrier, inc=1, device_id={"src": lax.rem(me_s + d, n_src)}, device_id_type=MESH)
        return 0

    lax.fori_loop(1, n_src, greet, 0)

    width = 2 * BINS
    moves[0].wait()
    both = folded[2:4].reshape(2 * rows, FOLD)
    moves[1].wait()
    p0 = dot(folded[0], dft[0])
    moves[2].wait()
    p1 = dot(both, dft[1])
    moves[3].wait()
    p2 = dot(folded[1], dft[2])
    moves[4].wait()
    p3 = dot(both, dft[3])
    parts = [
        p0[:, :BINS], p0[:, BINS:],
        p1[:rows, :BINS] + p1[rows:, BINS:], p1[:rows, BINS:] - p1[rows:, :BINS],
        p2[:, :BINS], p2[:, BINS:],
        p3[:rows, :BINS] - p3[rows:, BINS:], p3[:rows, BINS:] + p3[rows:, :BINS],
    ]
    spectra = jnp.concatenate(parts, axis=1)
    energy = jnp.sum(spectra * spectra, axis=1, keepdims=True) * (1.0 / (2 * NB))
    white = (spectra * (1.0 / jnp.sqrt(energy + 1e-06))).astype(jnp.bfloat16)
    row_slots[me_r] = white
    col_slots[me_s] = white

    pl.semaphore_wait(barrier, n_rcv - 1 + n_src - 1)

    def row_copy(to, slot):
        return pltpu.make_async_remote_copy(
            src_ref=row_slots.at[slot], dst_ref=row_slots.at[slot],
            send_sem=row_send.at[to], recv_sem=row_recv.at[slot],
            device_id={"rcv": to}, device_id_type=MESH,
        )

    def col_copy(to, slot, sem=None):
        return pltpu.make_async_remote_copy(
            src_ref=col_slots.at[slot], dst_ref=col_slots.at[slot],
            send_sem=col_send.at[to if sem is None else sem], recv_sem=col_recv.at[slot],
            device_id={"src": to}, device_id_type=MESH,
        )

    def send(d, _):
        col_copy(lax.rem(me_s + d, n_src), me_s).start()
        return 0

    if n_src == 4:
        col_copy(across, me_s).start()
        col_copy(near, me_s).start()

        @pl.when(jnp.logical_not(inner))
        def _():
            col_copy(far, me_s).start()
    else:
        lax.fori_loop(1, n_src, send, 0)

    for d in range(1, n_rcv):
        row_copy(lax.rem(me_r + d, n_rcv), me_r).start()

    if n_src == 4:
        @pl.when(inner)
        def _():
            col_copy(across, across).wait_recv()
            col_copy(near, across, far).start()

    for d in range(1, n_rcv):
        other = lax.rem(me_r + d, n_rcv)
        row_copy(other, other).wait_recv()
    for j in range(n_rcv):
        block = row_slots[j].astype(jnp.float32)
        for g in range(segs):
            sources[g, j * ch:(j + 1) * ch, :] = block[g * ch:(g + 1) * ch]

    n_here = n_rcv * ch

    def shard(p):
        receivers[...] = col_slots[p].astype(jnp.float32)
        cross = []
        for r in range(RADIX):
            at_re = slice(r * width, r * width + BINS)
            at_im = slice(r * width + BINS, (r + 1) * width)
            re = im = 0.0
            for g in range(segs):
                s_re = sources[g, :, at_re][None]
                s_im = sources[g, :, at_im][None]
                r_re = receivers[g * ch:(g + 1) * ch, at_re][:, None]
                r_im = receivers[g * ch:(g + 1) * ch, at_im][:, None]
                re = re + (s_re * r_re + s_im * r_im)
                im = im + (s_re * r_im - s_im * r_re)
            cross += [re.astype(jnp.bfloat16).reshape(ch * n_here, BINS), im.astype(jnp.bfloat16).reshape(ch * n_here, BINS)]
        done = dot(jnp.concatenate(cross, axis=1), lag[...]) * (1.0 / math.sqrt(segs * NB))
        corr[pl.ds(pl.multiple_of(p * ch * n_here, ch * n_here), ch * n_here), :] = done

    moves[5].wait()
    shard(me_s)

    def arrive(d, _):
        other = lax.rem(me_s + d, n_src)
        col_copy(other, other).wait_recv()
        shard(other)
        return 0

    if n_src == 4:
        col_copy(near, near).wait_recv()
        shard(near)

        @pl.when(jnp.logical_not(inner))
        def _():
            col_copy(across, across).wait_recv()

        shard(across)
        col_copy(far, far).wait_recv()
        shard(far)
    else:
        lax.fori_loop(1, n_src, arrive, 0)

    moves[6].wait()
    for s in range(n_here):
        placed[s] = dot(pick[...], corr[pl.ds(s, n_src * ch, stride=n_here), :].astype(jnp.bfloat16))

    for d in range(1, n_rcv):
        row_copy(lax.rem(me_r + d, n_rcv), me_r).wait_send()

    def sent(d, _):
        col_copy(lax.rem(me_s + d, n_src), me_s).wait_send()
        return 0

    lax.fori_loop(1, n_src, sent, 0)


def on_device(n_src, n_rcv, traces, offsets, receiver_slots):
    dft, lag = tables()
    ch = traces.shape[0]
    segs = offsets.shape[0]
    rows = segs * ch
    n_here, n_cols = n_rcv * ch, n_src * ch
    vmem = pl.BlockSpec(memory_space=pltpu.VMEM)
    anywhere = pl.BlockSpec(memory_space=pl.ANY)
    folded, pick = pl.pallas_call(
        functools.partial(fold, segs, ch),
        out_shape=[
            jax.ShapeDtypeStruct((RADIX, rows, FOLD), jnp.bfloat16),
            jax.ShapeDtypeStruct((n_cols, n_cols), jnp.bfloat16),
        ],
        in_specs=[anywhere] * 3,
        out_specs=[vmem] * 2,
        scratch_shapes=[
            pltpu.SMEM(offsets.shape, jnp.int32),
            pltpu.SMEM(receiver_slots.shape, jnp.int32),
            pltpu.VMEM(traces.shape, jnp.bfloat16),
            pltpu.VMEM((RADIX, rows, FOLD), jnp.float32),
            pltpu.VMEM((n_cols, n_cols), jnp.float32),
            pltpu.SemaphoreType.DMA((3,)),
        ],
    )(offsets, receiver_slots, traces)
    placed = pl.pallas_call(
        functools.partial(body, n_src, n_rcv, segs, ch),
        out_shape=jax.ShapeDtypeStruct((n_here, n_cols, LAGS), jnp.float32),
        in_specs=[anywhere] * 4,
        out_specs=vmem,
        scratch_shapes=[
            pltpu.VMEM((RADIX, rows, FOLD), jnp.bfloat16),
            pltpu.VMEM((n_cols, n_cols), jnp.bfloat16),
            pltpu.VMEM(dft.shape, jnp.bfloat16),
            pltpu.VMEM(lag.shape, jnp.bfloat16),
            pltpu.VMEM((n_rcv, rows, 2 * NB), jnp.bfloat16),
            pltpu.VMEM((n_src, rows, 2 * NB), jnp.bfloat16),
            pltpu.VMEM((segs, n_here, 2 * NB), jnp.float32),
            pltpu.VMEM((rows, 2 * NB), jnp.float32),
            pltpu.VMEM((n_here * n_cols, LAGS), jnp.float32),
            pltpu.SemaphoreType.DMA((RADIX + 3,)),
            pltpu.SemaphoreType.DMA((n_rcv,)),
            pltpu.SemaphoreType.DMA((n_rcv,)),
            pltpu.SemaphoreType.DMA((n_src,)),
            pltpu.SemaphoreType.DMA((n_src,)),
        ],
        compiler_params=pltpu.CompilerParams(collective_id=0, has_side_effects=True),
    )(folded, pick, jnp.asarray(dft), jnp.asarray(lag))
    return placed.astype(jnp.bfloat16)


def solution(mesh):
    in_specs = (P(("group", "src", "rcv"), None), P("group"), P(("group", "rcv"), None))
    out_specs = P(("group", "src"), "rcv", None)
    return jax.shard_map(
        functools.partial(on_device, mesh.shape["src"], mesh.shape["rcv"]),
        mesh=mesh, in_specs=in_specs, out_specs=out_specs, check_vma=False,
    )
```

```python
import functools
import math

import jax
import jax.numpy as jnp
import numpy as np
from jax import lax
from jax.experimental import pallas as pl
from jax.experimental.pallas import tpu as pltpu
from jax.sharding import PartitionSpec as P

SEG_LEN = 4096
NB = 512
LAGS = 128
LAG_STEP = 4
RADIX = 4
FOLD = SEG_LEN // RADIX
BINS = NB // RADIX
MESH = pl.DeviceIdType.MESH


def tables():
    k = RADIX * np.arange(BINS)[None, :] + np.arange(RADIX)[:, None]
    t = np.arange(FOLD)[:, None, None]
    dft = 2.0 * math.pi / SEG_LEN * ((t * k[None]) % SEG_LEN)
    dft = np.stack([np.cos(dft), -np.sin(dft)], axis=2).reshape(FOLD, RADIX, 2 * BINS).transpose(1, 0, 2)
    tau = LAG_STEP * (np.arange(LAGS) - LAGS // 2)
    lag = 2.0 * math.pi / SEG_LEN * ((k[:, :, None] * tau) % SEG_LEN)
    lag = np.stack([np.cos(lag), -np.sin(lag)], axis=1).reshape(2 * NB, LAGS)
    dft = dft.reshape(RADIX * FOLD, 2 * BINS)
    lag = lag.reshape(2, NB, LAGS).transpose(1, 0, 2).reshape(NB, 2 * LAGS)
    return np.concatenate([dft, lag], axis=0).astype(np.float32).astype(jnp.bfloat16)


def dot(left, right):
    return jnp.dot(left, right, preferred_element_type=jnp.float32)


def whiten(segs, ch, offsets_in, slots_in, traces_in, table, white, pick, offsets, slots, traces, dft, folded, chosen, in_sem):
    moves = [
        pltpu.make_async_copy(one, two, in_sem.at[i])
        for i, (one, two) in enumerate(
            [(offsets_in, offsets), (slots_in, slots), (traces_in, traces)]
            + [(table.at[r * FOLD:(r + 1) * FOLD], dft.at[r]) for r in range(RADIX)]
        )
    ]
    for move in moves:
        move.start()
    for move in moves[:2]:
        move.wait()

    n_cols = chosen.shape[1]
    place = lax.broadcasted_iota(jnp.int32, (1, n_cols), 1)

    def choose(q, _):
        chosen[pl.ds(q, 1), :] = jnp.where(place == slots[0, q], 1.0, 0.0)
        return 0

    lax.fori_loop(0, n_cols, choose, 0)
    pick[...] = chosen[...].astype(jnp.bfloat16)
    moves[2].wait()
    window = traces.shape[1]
    lane = lax.broadcasted_iota(jnp.int32, (ch, 128), 1)
    for g in range(segs):
        start = offsets[g]
        shift = lax.rem(start, 128)
        base = pl.multiple_of(start - shift, 128)
        last = pl.multiple_of(jnp.minimum(base + SEG_LEN, window - 128), 128)
        main = traces[:, pl.ds(base, SEG_LEN)].astype(jnp.float32)
        extra = traces[:, pl.ds(last, 128)].astype(jnp.float32)
        back = lax.rem(128 - shift, 128)
        turned = [pltpu.roll(main[:, j * 128:(j + 1) * 128], back, 1) for j in range(SEG_LEN // 128)]
        turned.append(pltpu.roll(extra, back, 1))
        keep = lane < 128 - shift
        piece = [jnp.where(keep, turned[j], turned[j + 1]) for j in range(SEG_LEN // 128)]
        step = FOLD // 128
        here = slice(g * ch, (g + 1) * ch)
        for j in range(step):
            x0, x1, x2, x3 = (piece[q * step + j] for q in range(RADIX))
            even, odd = x0 + x2, x1 + x3
            at = slice(j * 128, (j + 1) * 128)
            folded[0, here, at] = even + odd
            folded[1, here, at] = even - odd
            folded[2, here, at] = x0 - x2
            folded[3, here, at] = x1 - x3
    rows = segs * ch
    both = folded[2:4].reshape(2 * rows, FOLD).astype(jnp.bfloat16)
    moves[3].wait()
    p0 = dot(folded[0].astype(jnp.bfloat16), dft[0])
    moves[4].wait()
    p1 = dot(both, dft[1])
    moves[5].wait()
    p2 = dot(folded[1].astype(jnp.bfloat16), dft[2])
    moves[6].wait()
    p3 = dot(both, dft[3])
    parts = [
        p0[:, :BINS], p0[:, BINS:],
        p1[:rows, :BINS] + p1[rows:, BINS:], p1[:rows, BINS:] - p1[rows:, :BINS],
        p2[:, :BINS], p2[:, BINS:],
        p3[:rows, :BINS] - p3[rows:, BINS:], p3[:rows, BINS:] + p3[rows:, :BINS],
    ]
    spectra = jnp.concatenate(parts, axis=1)
    energy = jnp.sum(spectra * spectra, axis=1, keepdims=True) * (1.0 / (2 * NB))
    white[...] = (spectra * (1.0 / jnp.sqrt(energy + 1e-06))).astype(jnp.bfloat16)


def body(
    n_src, n_rcv, segs, ch,
    white, pick, table, out,
    lag, row_slots, col_slots, sources, receivers, corr,
    in_sem, row_send, row_recv, col_send, col_recv,
):
    me_r = lax.axis_index("rcv")
    me_s = lax.axis_index("src")
    rows = segs * ch
    near = me_s + 1 - 2 * lax.rem(me_s, 2)
    across = n_src - 1 - me_s
    far = lax.rem(me_s + 2, n_src)
    inner = lax.rem(me_s, 3) != 0

    moves = [
        pltpu.make_async_copy(one, two, in_sem.at[i])
        for i, (one, two) in enumerate(
            [(table.at[RADIX * FOLD:, h * LAGS:(h + 1) * LAGS], lag.at[h * NB:(h + 1) * NB]) for h in range(2)]
        )
    ]
    for move in moves:
        move.start()

    barrier = pltpu.get_barrier_semaphore()
    for d in range(1, n_rcv):
        pl.semaphore_signal(barrier, inc=1, device_id={"rcv": lax.rem(me_r + d, n_rcv)}, device_id_type=MESH)

    def greet(d, _):
        pl.semaphore_signal(barrier, inc=1, device_id={"src": lax.rem(me_s + d, n_src)}, device_id_type=MESH)
        return 0

    lax.fori_loop(1, n_src, greet, 0)

    row_slots[me_r] = white[...]
    col_slots[me_s] = white[...]
    pl.semaphore_wait(barrier, n_rcv - 1 + n_src - 1)

    def row_copy(to, slot):
        return pltpu.make_async_remote_copy(
            src_ref=row_slots.at[slot], dst_ref=row_slots.at[slot],
            send_sem=row_send.at[to], recv_sem=row_recv.at[slot],
            device_id={"rcv": to}, device_id_type=MESH,
        )

    def col_copy(to, slot, sem=None):
        return pltpu.make_async_remote_copy(
            src_ref=col_slots.at[slot], dst_ref=col_slots.at[slot],
            send_sem=col_send.at[to if sem is None else sem], recv_sem=col_recv.at[slot],
            device_id={"src": to}, device_id_type=MESH,
        )

    def send(d, _):
        col_copy(lax.rem(me_s + d, n_src), me_s).start()
        return 0

    if n_src == 4:
        @pl.when(inner)
        def _():
            col_copy(across, me_s).start()

        col_copy(near, me_s).start()
    else:
        lax.fori_loop(1, n_src, send, 0)

    for d in range(1, n_rcv):
        row_copy(lax.rem(me_r + d, n_rcv), me_r).start()

    if n_src == 4:
        @pl.when(inner)
        def _():
            col_copy(across, across).wait_recv()
            col_copy(near, across, far).start()

        @pl.when(jnp.logical_not(inner))
        def _():
            col_copy(near, me_s).wait_send()
            col_copy(across, me_s).start()
            col_copy(far, me_s).start()

    for d in range(1, n_rcv):
        other = lax.rem(me_r + d, n_rcv)
        row_copy(other, other).wait_recv()
    for j in range(n_rcv):
        block = row_slots[j].astype(jnp.float32)
        for g in range(segs):
            sources[g, j * ch:(j + 1) * ch, :] = block[g * ch:(g + 1) * ch]

    n_here = n_rcv * ch
    width = 2 * BINS

    def shard(p):
        receivers[...] = col_slots[p].astype(jnp.float32)
        cross = []
        for r in range(RADIX):
            at_re = slice(r * width, r * width + BINS)
            at_im = slice(r * width + BINS, (r + 1) * width)
            re = im = 0.0
            for g in range(segs):
                s_re = sources[g, :, at_re][None]
                s_im = sources[g, :, at_im][None]
                r_re = receivers[g * ch:(g + 1) * ch, at_re][:, None]
                r_im = receivers[g * ch:(g + 1) * ch, at_im][:, None]
                re = re + (s_re * r_re + s_im * r_im)
                im = im + (s_re * r_im - s_im * r_re)
            cross += [re.astype(jnp.bfloat16).reshape(ch * n_here, BINS), im.astype(jnp.bfloat16).reshape(ch * n_here, BINS)]
        done = dot(jnp.concatenate(cross, axis=1), lag[...]) * (1.0 / math.sqrt(segs * NB))
        corr[pl.ds(pl.multiple_of(p * ch * n_here, ch * n_here), ch * n_here), :] = done

    for move in moves:
        move.wait()
    shard(me_s)

    def arrive(d, _):
        other = lax.rem(me_s + d, n_src)
        col_copy(other, other).wait_recv()
        shard(other)
        return 0

    if n_src == 4:
        col_copy(near, near).wait_recv()
        shard(near)

        @pl.when(jnp.logical_not(inner))
        def _():
            col_copy(across, across).wait_recv()

        shard(across)
        col_copy(far, far).wait_recv()
        shard(far)
    else:
        lax.fori_loop(1, n_src, arrive, 0)

    for s in range(n_here):
        out[s] = dot(pick[...], corr[pl.ds(s, n_src * ch, stride=n_here), :].astype(jnp.bfloat16)).astype(jnp.bfloat16)

    for d in range(1, n_rcv):
        row_copy(lax.rem(me_r + d, n_rcv), me_r).wait_send()

    def sent(d, _):
        col_copy(lax.rem(me_s + d, n_src), me_s).wait_send()
        return 0

    if n_src == 4:
        @pl.when(inner)
        def _():
            col_copy(near, me_s).wait_send()

        col_copy(across, me_s).wait_send()
        col_copy(far, me_s).wait_send()
    else:
        lax.fori_loop(1, n_src, sent, 0)


def on_device(n_src, n_rcv, traces, offsets, receiver_slots):
    table = jnp.asarray(tables())
    ch = traces.shape[0]
    segs = offsets.shape[0]
    rows = segs * ch
    n_here, n_cols = n_rcv * ch, n_src * ch
    vmem = pl.BlockSpec(memory_space=pltpu.VMEM)
    hbm = pl.BlockSpec(memory_space=pltpu.HBM)
    room = 40 * 1024 * 1024
    white, pick = pl.pallas_call(
        functools.partial(whiten, segs, ch),
        out_shape=[
            jax.ShapeDtypeStruct((rows, 2 * NB), jnp.bfloat16),
            jax.ShapeDtypeStruct((n_cols, n_cols), jnp.bfloat16),
        ],
        in_specs=[hbm] * 4,
        out_specs=[vmem] * 2,
        scratch_shapes=[
            pltpu.SMEM(offsets.shape, jnp.int32),
            pltpu.SMEM(receiver_slots.shape, jnp.int32),
            pltpu.VMEM(traces.shape, jnp.bfloat16),
            pltpu.VMEM((RADIX, FOLD, 2 * BINS), jnp.bfloat16),
            pltpu.VMEM((RADIX, rows, FOLD), jnp.float32),
            pltpu.VMEM((n_cols, n_cols), jnp.float32),
            pltpu.SemaphoreType.DMA((RADIX + 3,)),
        ],
        compiler_params=pltpu.CompilerParams(vmem_limit_bytes=room),
    )(offsets, receiver_slots, traces, table)
    return pl.pallas_call(
        functools.partial(body, n_src, n_rcv, segs, ch),
        out_shape=jax.ShapeDtypeStruct((n_here, n_cols, LAGS), jnp.bfloat16),
        in_specs=[vmem, vmem, hbm],
        out_specs=vmem,
        scratch_shapes=[
            pltpu.VMEM((2 * NB, LAGS), jnp.bfloat16),
            pltpu.VMEM((n_rcv, rows, 2 * NB), jnp.bfloat16),
            pltpu.VMEM((n_src, rows, 2 * NB), jnp.bfloat16),
            pltpu.VMEM((segs, n_here, 2 * NB), jnp.float32),
            pltpu.VMEM((rows, 2 * NB), jnp.float32),
            pltpu.VMEM((n_here * n_cols, LAGS), jnp.float32),
            pltpu.SemaphoreType.DMA((2,)),
            pltpu.SemaphoreType.DMA((n_rcv,)),
            pltpu.SemaphoreType.DMA((n_rcv,)),
            pltpu.SemaphoreType.DMA((n_src,)),
            pltpu.SemaphoreType.DMA((n_src,)),
        ],
        compiler_params=pltpu.CompilerParams(
            collective_id=0, has_side_effects=True, vmem_limit_bytes=room
        ),
    )(white, pick, table)


def solution(mesh):
    in_specs = (P(("group", "src", "rcv"), None), P("group"), P(("group", "rcv"), None))
    out_specs = P(("group", "src"), "rcv", None)
    return jax.shard_map(
        functools.partial(on_device, mesh.shape["src"], mesh.shape["rcv"]),
        mesh=mesh, in_specs=in_specs, out_specs=out_specs, check_vma=False,
    )
```

```python
import functools
import math

import jax
import jax.numpy as jnp
import numpy as np
from jax import lax
from jax.experimental import pallas as pl
from jax.experimental.pallas import tpu as pltpu
from jax.sharding import PartitionSpec as P

SEG_LEN = 4096
NB = 512
LAGS = 128
LAG_STEP = 4
RADIX = 4
FOLD = SEG_LEN // RADIX
BINS = NB // RADIX
MESH = pl.DeviceIdType.MESH


def tables():
    k = RADIX * np.arange(BINS)[None, :] + np.arange(RADIX)[:, None]
    t = np.arange(FOLD)[:, None, None]
    dft = 2.0 * math.pi / SEG_LEN * ((t * k[None]) % SEG_LEN)
    dft = np.stack([np.cos(dft), -np.sin(dft)], axis=2).reshape(FOLD, RADIX, 2 * BINS).transpose(1, 0, 2)
    tau = LAG_STEP * (np.arange(LAGS) - LAGS // 2)
    lag = 2.0 * math.pi / SEG_LEN * ((k[:, :, None] * tau) % SEG_LEN)
    lag = np.stack([np.cos(lag), -np.sin(lag)], axis=1).reshape(2 * NB, LAGS)
    dft = dft.reshape(RADIX * FOLD, 2 * BINS)
    lag = lag.reshape(2, NB, LAGS).transpose(1, 0, 2).reshape(NB, 2 * LAGS)
    return np.concatenate([dft, lag], axis=0).astype(np.float32).astype(jnp.bfloat16)


def dot(left, right):
    return jnp.dot(left, right, preferred_element_type=jnp.float32)


def whiten(segs, ch, offsets_in, slots_in, traces_in, table, white, pick, offsets, slots, traces, dft, folded, chosen, in_sem):
    moves = [
        pltpu.make_async_copy(one, two, in_sem.at[i])
        for i, (one, two) in enumerate(
            [(offsets_in, offsets), (slots_in, slots), (traces_in, traces)]
            + [(table.at[r * FOLD:(r + 1) * FOLD], dft.at[r]) for r in range(RADIX)]
        )
    ]
    for move in moves:
        move.start()
    for move in moves[:2]:
        move.wait()

    n_cols = chosen.shape[1]
    place = lax.broadcasted_iota(jnp.int32, (1, n_cols), 1)

    def choose(q, _):
        chosen[pl.ds(q, 1), :] = jnp.where(place == slots[0, q], 1.0, 0.0)
        return 0

    lax.fori_loop(0, n_cols, choose, 0)
    pick[...] = chosen[...].astype(jnp.bfloat16)
    moves[2].wait()
    window = traces.shape[1]
    lane = lax.broadcasted_iota(jnp.int32, (ch, 128), 1)
    for g in range(segs):
        start = offsets[g]
        shift = lax.rem(start, 128)
        base = pl.multiple_of(start - shift, 128)
        last = pl.multiple_of(jnp.minimum(base + SEG_LEN, window - 128), 128)
        main = traces[:, pl.ds(base, SEG_LEN)].astype(jnp.float32)
        extra = traces[:, pl.ds(last, 128)].astype(jnp.float32)
        back = lax.rem(128 - shift, 128)
        turned = [pltpu.roll(main[:, j * 128:(j + 1) * 128], back, 1) for j in range(SEG_LEN // 128)]
        turned.append(pltpu.roll(extra, back, 1))
        keep = lane < 128 - shift
        piece = [jnp.where(keep, turned[j], turned[j + 1]) for j in range(SEG_LEN // 128)]
        step = FOLD // 128
        here = slice(g * ch, (g + 1) * ch)
        for j in range(step):
            x0, x1, x2, x3 = (piece[q * step + j] for q in range(RADIX))
            even, odd = x0 + x2, x1 + x3
            at = slice(j * 128, (j + 1) * 128)
            folded[0, here, at] = even + odd
            folded[1, here, at] = even - odd
            folded[2, here, at] = x0 - x2
            folded[3, here, at] = x1 - x3
    rows = segs * ch
    both = folded[2:4].reshape(2 * rows, FOLD).astype(jnp.bfloat16)
    moves[3].wait()
    p0 = dot(folded[0].astype(jnp.bfloat16), dft[0])
    moves[4].wait()
    p1 = dot(both, dft[1])
    moves[5].wait()
    p2 = dot(folded[1].astype(jnp.bfloat16), dft[2])
    moves[6].wait()
    p3 = dot(both, dft[3])
    parts = [
        p0[:, :BINS], p0[:, BINS:],
        p1[:rows, :BINS] + p1[rows:, BINS:], p1[:rows, BINS:] - p1[rows:, :BINS],
        p2[:, :BINS], p2[:, BINS:],
        p3[:rows, :BINS] - p3[rows:, BINS:], p3[:rows, BINS:] + p3[rows:, :BINS],
    ]
    spectra = jnp.concatenate(parts, axis=1)
    energy = jnp.sum(spectra * spectra, axis=1, keepdims=True) * (1.0 / (2 * NB))
    white[...] = (spectra * (1.0 / jnp.sqrt(energy + 1e-06))).astype(jnp.bfloat16)


def body(
    n_src, n_rcv, segs, ch,
    white, pick_in, table, out,
    pick, lag, row_slots, col_slots, sources, receivers, corr,
    in_sem, row_send, row_recv, col_send, col_recv,
):
    me_r = lax.axis_index("rcv")
    me_s = lax.axis_index("src")
    rows = segs * ch
    near = me_s + 1 - 2 * lax.rem(me_s, 2)
    across = n_src - 1 - me_s
    far = lax.rem(me_s + 2, n_src)
    inner = (lax.rem(me_s, 3) + 1) // 2
    second = far + inner * (across - far)
    third = across + inner * (far - across)

    moves = [
        pltpu.make_async_copy(one, two, in_sem.at[i])
        for i, (one, two) in enumerate(
            [(white, col_slots.at[me_s]), (white, row_slots.at[me_r]), (pick_in, pick)]
            + [(table.at[RADIX * FOLD:, h * LAGS:(h + 1) * LAGS], lag.at[h * NB:(h + 1) * NB]) for h in range(2)]
        )
    ]
    for move in moves:
        move.start()

    barrier = pltpu.get_barrier_semaphore()
    for d in range(1, n_rcv):
        pl.semaphore_signal(barrier, inc=1, device_id={"rcv": lax.rem(me_r + d, n_rcv)}, device_id_type=MESH)

    def greet(d, _):
        pl.semaphore_signal(barrier, inc=1, device_id={"src": lax.rem(me_s + d, n_src)}, device_id_type=MESH)
        return 0

    lax.fori_loop(1, n_src, greet, 0)

    moves[0].wait()
    moves[1].wait()
    pl.semaphore_wait(barrier, n_rcv - 1 + n_src - 1)

    def row_copy(to, slot):
        return pltpu.make_async_remote_copy(
            src_ref=row_slots.at[slot], dst_ref=row_slots.at[slot],
            send_sem=row_send.at[to], recv_sem=row_recv.at[slot],
            device_id={"rcv": to}, device_id_type=MESH,
        )

    def col_copy(to, slot):
        return pltpu.make_async_remote_copy(
            src_ref=col_slots.at[slot], dst_ref=col_slots.at[slot],
            send_sem=col_send.at[to], recv_sem=col_recv.at[slot],
            device_id={"src": to}, device_id_type=MESH,
        )

    def send(d, _):
        col_copy(lax.rem(me_s + d, n_src), me_s).start()
        return 0

    if n_src == 4:
        for to in (across, far, near):
            col_copy(to, me_s).start()
    else:
        lax.fori_loop(1, n_src, send, 0)

    for d in range(1, n_rcv):
        row_copy(lax.rem(me_r + d, n_rcv), me_r).start()

    for d in range(1, n_rcv):
        other = lax.rem(me_r + d, n_rcv)
        row_copy(other, other).wait_recv()
    for j in range(n_rcv):
        block = row_slots[j].astype(jnp.float32)
        for g in range(segs):
            sources[g, j * ch:(j + 1) * ch, :] = block[g * ch:(g + 1) * ch]

    n_here = n_rcv * ch
    width = 2 * BINS

    def shard(p):
        receivers[...] = col_slots[p].astype(jnp.float32)
        cross = []
        for r in range(RADIX):
            at_re = slice(r * width, r * width + BINS)
            at_im = slice(r * width + BINS, (r + 1) * width)
            re = im = 0.0
            for g in range(segs):
                s_re = sources[g, :, at_re][None]
                s_im = sources[g, :, at_im][None]
                r_re = receivers[g * ch:(g + 1) * ch, at_re][:, None]
                r_im = receivers[g * ch:(g + 1) * ch, at_im][:, None]
                re = re + (s_re * r_re + s_im * r_im)
                im = im + (s_re * r_im - s_im * r_re)
            cross += [re.astype(jnp.bfloat16).reshape(ch * n_here, BINS), im.astype(jnp.bfloat16).reshape(ch * n_here, BINS)]
        done = dot(jnp.concatenate(cross, axis=1), lag[...]) * (1.0 / math.sqrt(segs * NB))
        corr[pl.ds(pl.multiple_of(p * ch * n_here, ch * n_here), ch * n_here), :] = done

    for move in moves[2:]:
        move.wait()
    shard(me_s)

    def arrive(d, _):
        other = lax.rem(me_s + d, n_src)
        col_copy(other, other).wait_recv()
        shard(other)
        return 0

    if n_src == 4:
        for other in (near, second, third):
            col_copy(other, other).wait_recv()
            shard(other)
    else:
        lax.fori_loop(1, n_src, arrive, 0)

    for s in range(n_here):
        out[s] = dot(pick[...], corr[pl.ds(s, n_src * ch, stride=n_here), :].astype(jnp.bfloat16)).astype(jnp.bfloat16)

    for d in range(1, n_rcv):
        row_copy(lax.rem(me_r + d, n_rcv), me_r).wait_send()

    def sent(d, _):
        col_copy(lax.rem(me_s + d, n_src), me_s).wait_send()
        return 0

    lax.fori_loop(1, n_src, sent, 0)


def on_device(n_src, n_rcv, traces, offsets, receiver_slots):
    table = jnp.asarray(tables())
    ch = traces.shape[0]
    segs = offsets.shape[0]
    rows = segs * ch
    n_here, n_cols = n_rcv * ch, n_src * ch
    vmem = pl.BlockSpec(memory_space=pltpu.VMEM)
    anywhere = pl.BlockSpec(memory_space=pl.ANY)
    white, pick = pl.pallas_call(
        functools.partial(whiten, segs, ch),
        out_shape=[
            jax.ShapeDtypeStruct((rows, 2 * NB), jnp.bfloat16),
            jax.ShapeDtypeStruct((n_cols, n_cols), jnp.bfloat16),
        ],
        in_specs=[anywhere] * 4,
        out_specs=[vmem] * 2,
        scratch_shapes=[
            pltpu.SMEM(offsets.shape, jnp.int32),
            pltpu.SMEM(receiver_slots.shape, jnp.int32),
            pltpu.VMEM(traces.shape, jnp.bfloat16),
            pltpu.VMEM((RADIX, FOLD, 2 * BINS), jnp.bfloat16),
            pltpu.VMEM((RADIX, rows, FOLD), jnp.float32),
            pltpu.VMEM((n_cols, n_cols), jnp.float32),
            pltpu.SemaphoreType.DMA((RADIX + 3,)),
        ],
    )(offsets, receiver_slots, traces, table)
    return pl.pallas_call(
        functools.partial(body, n_src, n_rcv, segs, ch),
        out_shape=jax.ShapeDtypeStruct((n_here, n_cols, LAGS), jnp.bfloat16),
        in_specs=[anywhere] * 3,
        out_specs=vmem,
        scratch_shapes=[
            pltpu.VMEM((n_cols, n_cols), jnp.bfloat16),
            pltpu.VMEM((2 * NB, LAGS), jnp.bfloat16),
            pltpu.VMEM((n_rcv, rows, 2 * NB), jnp.bfloat16),
            pltpu.VMEM((n_src, rows, 2 * NB), jnp.bfloat16),
            pltpu.VMEM((segs, n_here, 2 * NB), jnp.float32),
            pltpu.VMEM((rows, 2 * NB), jnp.float32),
            pltpu.VMEM((n_here * n_cols, LAGS), jnp.float32),
            pltpu.SemaphoreType.DMA((5,)),
            pltpu.SemaphoreType.DMA((n_rcv,)),
            pltpu.SemaphoreType.DMA((n_rcv,)),
            pltpu.SemaphoreType.DMA((n_src,)),
            pltpu.SemaphoreType.DMA((n_src,)),
        ],
        compiler_params=pltpu.CompilerParams(collective_id=0, has_side_effects=True),
    )(white, pick, table)


def solution(mesh):
    in_specs = (P(("group", "src", "rcv"), None), P("group"), P(("group", "rcv"), None))
    out_specs = P(("group", "src"), "rcv", None)
    return jax.shard_map(
        functools.partial(on_device, mesh.shape["src"], mesh.shape["rcv"]),
        mesh=mesh, in_specs=in_specs, out_specs=out_specs, check_vma=False,
    )
```
